32 devices in a mesh: tok: 4 (over x, core), head: 8 (over z, y).
Axes of the slice: x: 2, y: 2, z: 4, core: 2. Of those that a mesh axis runs over, the one named last changes fastest.
Arguments:
- q_nope: bfloat16 [512, 16384], P('tok', 'head'), may hold values from -6 to 6
- q_rope: bfloat16 [512, 8192], P('tok', 'head'), may hold values from -10 to 10
- cache_kv: bfloat16 [512, 576], P('tok'), may hold values from -6 to 6
- span_kv: bfloat16 [512, 576], P('tok'), may hold values from -6 to 6
- w_uk: bfloat16 [512, 16384], P(None, 'head'), may hold values from -0.5 to 0.5
- w_uv: bfloat16 [512, 16384], P(None, 'head'), may hold values from -3 to 3
- w_o: bfloat16 [16384, 7168], P('head', 'tok'), may hold values from -0.046875 to 0.046875
- prefix_length: int32 [1], replicated, may hold values from 256 to 512
Outputs:
- attn_out: bfloat16 [512, 7168], P('head', 'tok')
The draws below stay inside these ranges and needn't reach their ends.
All inputs are finite; a program needn't handle non-finite values.
Results may differ from the reference program's by a relative error of at most 0.014.
Values may be sent and summed in bfloat16 or wider, within the bound.
No kernel may reach another device: no remote copies, remote signals or barrier semaphores. Data moves between devices by JAX's collectives and lax.ppermute only.
A program may use at most 64 MiB of HBM per device.

```python
import math
import jax
import jax.numpy as jnp
from jax import lax

D = 7168
H = 128
DN = 128
DR = 64
DV = 128
KVL = 512
SPAN = 512
PREFIX = 512


def draw_cache_kv(key, part):
    key = jax.random.fold_in(key, 11)
    base_values = jax.random.normal(key, (PREFIX, KVL + DR), jnp.float32)
    return jnp.clip(base_values, -6.0, 6.0).astype(jnp.bfloat16)


def draw_q_rope(key, part):
    key = jax.random.fold_in(key, 23)
    base_values = jax.random.normal(key, (SPAN, H * DR), jnp.float32)
    return jnp.clip(base_values, -6.0, 6.0).astype(jnp.bfloat16)


def shard_levels(own_key, extent, pieces, least, largest):
    def one(axis_at, parts):
        steps = jax.random.uniform(jax.random.fold_in(jax.random.fold_in(own_key, 6), axis_at), (parts,), jnp.float32, least / len(pieces), largest / len(pieces))
        return jnp.repeat(jnp.exp(steps), extent[axis_at] // parts).reshape((-1,) + (1,) * (len(extent) - axis_at - 1))

    gain = one(*pieces[0])
    for cut in pieces[1:]:
        gain = gain * one(*cut)
    return gain


def gaussian(rng, extent, spread, most, shards=(), held_as=jnp.bfloat16):
    result = spread * jax.random.normal(rng, extent, jnp.float32)
    if shards:
        result = result * shard_levels(rng, extent, shards, -0.22, 0.18)
    return jnp.clip(result, -most, most).astype(held_as)


def setup_inputs(seed: int = 0) -> dict:
    key_list = jax.random.split(jax.random.key(seed), 9)
    return {
        "q_nope": gaussian(key_list[0], (SPAN, H * DN), 1.0, 6.0, ((0, 4), (1, 8))),
        "q_rope": draw_q_rope(jax.random.fold_in(key_list[8], 71), 0),
        "cache_kv": draw_cache_kv(jax.random.fold_in(key_list[8], 71), 0),
        "span_kv": gaussian(key_list[3], (SPAN, KVL + DR), 1.0, 6.0, ((0, 4),)),
        "w_uk": gaussian(key_list[4], (KVL, H * DN), DN ** -0.5, 0.5, ((1, 8),)),
        "w_uv": gaussian(key_list[5], (KVL, H * DV), 0.5, 3.0, ((1, 8),)),
        "w_o": gaussian(key_list[6], (H * DV, D), (H * DV) ** -0.5, 0.046875, ((0, 8), (1, 4))),
        "prefix_length": jax.random.randint(key_list[7], (1,), PREFIX // 2, PREFIX + 1).astype(jnp.int32),
    }


MASKED = -1e+30

def reference(q_nope, q_rope, cache_kv, span_kv, w_uk, w_uv, w_o, prefix_length):
    keys = jnp.concatenate([cache_kv, span_kv], 0)
    key_latent = keys[:, :KVL]
    key_rotary = keys[:, KVL:]
    score_scale = 1.0 / math.sqrt(DN + DR)
    query_latent = jnp.einsum('thn,khn->thk', q_nope.reshape(SPAN, H, DN).astype(jnp.float32), w_uk.reshape(KVL, H, DN).astype(jnp.float32)).astype(jnp.bfloat16)
    query_rotary = q_rope.reshape(SPAN, H, DR)
    key_pos = jnp.arange(PREFIX + SPAN, dtype=jnp.int32)
    token_pos = jnp.arange(SPAN, dtype=jnp.int32)
    cache_live = key_pos < prefix_length[0]
    span_live = key_pos[None, :] - PREFIX <= token_pos[:, None]
    is_live = jnp.where((key_pos < PREFIX)[None, :], cache_live[None, :], span_live)

    def one_head(inputs):
        head_latent, head_rotary = inputs
        scores = jnp.dot(head_latent, key_latent.T, preferred_element_type=jnp.float32)
        scores = scores + jnp.dot(head_rotary, key_rotary.T, preferred_element_type=jnp.float32)
        scores = jnp.where(is_live, scores * score_scale, MASKED)
        top_score = lax.optimization_barrier(jnp.max(scores, axis=1, keepdims=True))
        weights = jnp.where(is_live, jnp.exp(scores - top_score), 0.0)
        weight_sum = lax.optimization_barrier(jnp.sum(weights, axis=1, keepdims=True))
        summed = jnp.dot(weights.astype(jnp.bfloat16), key_latent, preferred_element_type=jnp.float32)
        return (summed / weight_sum).astype(jnp.bfloat16)
    latent_out = lax.map(one_head, (jnp.transpose(query_latent, (1, 0, 2)), jnp.transpose(query_rotary, (1, 0, 2))))
    value_out = jnp.einsum('htk,khv->thv', latent_out.astype(jnp.float32), w_uv.reshape(KVL, H, DV).astype(jnp.float32)).astype(jnp.bfloat16)
    return jnp.dot(value_out.reshape(SPAN, H * DV), w_o, preferred_element_type=jnp.float32).astype(jnp.bfloat16)
```

```python
import functools
import math

import jax
import jax.numpy as jnp
from jax import lax
from jax.experimental import pallas as pl
from jax.experimental.pallas import tpu as pltpu
from jax.sharding import PartitionSpec as P

DN = 128
DR = 64
DV = 128
KVL = 512
KD = KVL + DR

MASKED = -1e30
CHUNKS = 2
FIRST = 0.72
COST_SHARE = 1
VMEM_LIMIT = 24 * 1024 * 1024
EXP_SCALE = math.log2(math.e) / math.sqrt(DN + DR)

f32 = jnp.float32
bf16 = jnp.bfloat16


def dot(a, b):
    return jnp.dot(a, b, preferred_element_type=f32)


def dot_t(a, b):
    return lax.dot_general(a, b, (((1,), (1,)), ((), ())), preferred_element_type=f32)


def xor_permute(x, axis, bit):
    n = lax.axis_size(axis)
    return lax.ppermute(x, axis, [(i, i ^ bit) for i in range(n)])


def bits_of(n):
    return [1 << i for i in range(n.bit_length() - 1)]


def in_vmem(x):
    return pltpu.with_memory_space_constraint(x, pltpu.VMEM)


def load_keys(caches, spans, rels, limit, tokens, kt, k, bias):
    me = lax.axis_index("tok")
    rows = bias.shape[0]
    half = tokens // 2
    part = half // CHUNKS
    row = lax.broadcasted_iota(jnp.int32, (rows, 1), 0)
    chunk, rest = row // (rows // CHUNKS), row % (rows // CHUNKS)
    token = (rest // part) * half + chunk * part + rest % part
    cached = caches[0].shape[1]
    size = cached + tokens
    for at, (cache, span, rel) in enumerate(zip(caches, spans, rels)):
        owner = me ^ rel
        start = at * size
        kt[:, start : start + cached] = cache[...]
        kt[:, start + cached : start + size] = span[...]
        column = lax.broadcasted_iota(jnp.int32, (rows, cached), 1)
        bias[:, start : start + cached] = jnp.where(owner * cached + column < limit, 0.0, MASKED)
        column = lax.broadcasted_iota(jnp.int32, (rows, tokens), 1)
        bias[:, start + cached : start + size] = jnp.where(
            owner * tokens + column <= me * tokens + token, 0.0, MASKED
        )
    k[...] = kt[:KVL, :].T


def split_refs(refs, *counts):
    out, at = [], 0
    for count in counts:
        out.append(refs[at : at + count])
        at += count
    return out + [refs[at:]]


def query_kernel(tokens, group, qn, qr, wuk, q_out, nope, rotary, up, sems):
    half = tokens // 2
    part = half // CHUNKS
    rows = tokens // CHUNKS
    steps = q_out.shape[1] // group

    def copies(i):
        wide = pl.ds(pl.multiple_of(i * group * DN, group * DN), group * DN)
        narrow = pl.ds(pl.multiple_of(i * group * DR, group * DR), group * DR)
        return [
            pltpu.make_async_copy(src.at[:, at], dst.at[:, at], sems.at[i, j])
            for j, (src, dst, at) in enumerate(
                ((wuk, up, wide), (qn, nope, wide), (qr, rotary, narrow))
            )
        ]

    for i in range(steps):
        for copy in copies(i):
            copy.start()

    def ordered(x):
        return jnp.concatenate(
            [
                x[b * half + c * part : b * half + (c + 1) * part]
                for c in range(CHUNKS)
                for b in range(2)
            ],
            0,
        )

    def step(i, _):
        for copy in copies(i):
            copy.wait()
        wide = pl.ds(pl.multiple_of(i * group * DN, group * DN), group * DN)
        narrow = pl.ds(pl.multiple_of(i * group * DR, group * DR), group * DR)
        n, r, w = nope[:, wide], rotary[:, narrow], up[:, wide]
        for g in range(group):
            latent = dot_t(n[:, g * DN : (g + 1) * DN], w[:, g * DN : (g + 1) * DN])
            latent = ordered(latent.astype(bf16))
            rope = ordered(r[:, g * DR : (g + 1) * DR])
            for c in range(CHUNKS):
                q_out[c, i * group + g, :, :KVL] = latent[c * rows : (c + 1) * rows]
                q_out[c, i * group + g, :, KVL:] = rope[c * rows : (c + 1) * rows]
        return 0

    lax.fori_loop(0, steps, step, 0)


def local_kernel(rels, tokens, group, *refs):
    n = len(rels)
    (limit, q), caches, spans, (acc_out, ml_out), (kt, k, bias) = split_refs(refs, 2, n, n, 2)
    load_keys(caches, spans, rels, limit[0], tokens, kt, k, bias)
    rows = tokens // CHUNKS
    keys = kt.shape[1]
    steps = q.shape[1] // group

    def step(i, _):
        c = i // steps
        heads = pl.ds((i % steps) * group, group)
        s = dot(q[c, heads].reshape(group * rows, KD), kt[...]).reshape(group, rows, keys)
        s = s + bias[pl.ds(pl.multiple_of(c * rows, rows), rows)][None]
        m = jnp.max(s, axis=2, keepdims=True)
        p = jnp.exp2((s - m) * EXP_SCALE)
        l = jnp.sum(p, axis=2, keepdims=True)
        o = dot(p.astype(bf16).reshape(group * rows, keys), k[...])
        lane = lax.broadcasted_iota(jnp.int32, (group, rows, 128), 2)
        acc_out[c, heads] = o.reshape(group, rows, KVL)
        ml_out[c, heads] = jnp.where(lane < 64, m, l)
        return 0

    lax.fori_loop(0, CHUNKS * steps, step, 0)


def rest_kernel(rels, tokens, group, which, *refs):
    n = len(rels)
    (limit, q, acc, ml, wuv), caches, spans, (out,), (kt, k, bias) = split_refs(refs, 5, n, n, 1)
    rows = tokens // CHUNKS
    load_keys(caches, spans, rels, limit[0], tokens, kt, k, bias)
    keys = kt.shape[1]

    def step(i, _):
        heads = pl.ds(i * group, group)
        columns = pl.ds(pl.multiple_of(i * group * DV, group * DV), group * DV)
        s = dot(q[which, heads].reshape(group * rows, KD), kt[...]).reshape(group, rows, keys)
        s = s + bias[which * rows : (which + 1) * rows][None]
        both = ml[which, heads]
        m1 = both[:, :, :1]
        l1 = both[:, :, 64:65]
        m = jnp.maximum(m1, jnp.max(s, axis=2, keepdims=True))
        p = jnp.exp2((s - m) * EXP_SCALE)
        a = jnp.exp2((m1 - m) * EXP_SCALE)
        l = l1 * a + jnp.sum(p, axis=2, keepdims=True)
        o = dot(p.astype(bf16).reshape(group * rows, keys), k[...]).reshape(group, rows, KVL)
        o = ((acc[which, heads] * a + o) / l).astype(bf16)
        up = wuv[:, columns]
        out[:, columns] = jnp.concatenate(
            [dot(o[g], up[:, g * DV : (g + 1) * DV]).astype(bf16) for g in range(group)], 1
        )
        return 0

    lax.fori_loop(0, q.shape[1] // group, step, 0)


def first_last(bits):
    if not bits:
        return [0]
    rest = first_last(bits[1:])
    return [bits[0] | x for x in rest] + rest


def project_kernel(n_tok, per, groups, *refs):
    pieces, (w_o,), outs, (lhs,) = split_refs(refs, n_tok, 1, 2 * len(groups))
    part = pieces[0].shape[0] // per
    n = n_tok * per
    bits = groups[0][0]
    order = first_last(bits)
    me_tok, me_head = lax.axis_index("tok"), lax.axis_index("head")
    for i in range(n_tok):
        for b in range(per):
            rel = ((me_tok ^ i) * per + b) ^ me_head
            at = jnp.int32(0)
            for step, bit in enumerate(bits):
                at = at + jnp.where(rel & bit == 0, n >> (step + 1), 0)
            start = pl.multiple_of(at * part, part)
            lhs[pl.ds(start, part), :] = pieces[i][b * part : (b + 1) * part, :]
    rows = n * part // 2
    for j, (own, start, count, tile) in enumerate(groups):
        send, keep = outs[2 * j : 2 * j + 2]
        for t in range(count):
            columns = slice((start + t) * tile, (start + t + 1) * tile)
            here = slice(t * tile, (t + 1) * tile)
            y = dot(lhs[...], w_o[:, columns]).astype(bf16)
            if own != bits:
                y = jnp.concatenate(
                    [y[order.index(r) * part :][:part] for r in first_last(own)], 0
                )
            send[:, here] = y[:rows]
            keep[:, here] = y[rows:]


def shards(q_nope, q_rope, cache_kv, span_kv, w_uk, w_uv, w_o, prefix_length):
    tokens = q_nope.shape[0]
    heads = w_uk.shape[1] // DN
    cache_rows = cache_kv.shape[0]
    n_tok, n_head = lax.axis_size("tok"), lax.axis_size("head")
    per = n_head // n_tok
    rows = tokens // CHUNKS
    params = pltpu.CompilerParams(vmem_limit_bytes=VMEM_LIMIT)
    smem = pl.BlockSpec(memory_space=pltpu.SMEM)
    vmem = pl.BlockSpec(memory_space=pltpu.VMEM)

    def step(held, axis_bit):
        return {rel ^ axis_bit: xor_permute(v, "tok", axis_bit) for rel, v in held.items()}

    def gather(x):
        held = {0: x}
        for bit in reversed(bits_of(n_tok)):
            held.update(step(held, bit))
        return [in_vmem(held[rel]) for rel in range(n_tok)]

    def cost(flops):
        return pl.CostEstimate(flops=flops // COST_SHARE, bytes_accessed=0, transcendentals=0)

    held = {0: (cache_kv.T, span_kv.T)}

    def key_step(held, bit):
        return {
            rel ^ bit: tuple(xor_permute(v, "tok", bit) for v in both)
            for rel, both in held.items()
        }

    for bit in reversed(bits_of(n_tok)[1:]):
        held.update(key_step(held, bit))
    held.update(key_step({0: held[0]}, 1))
    caches = {rel: in_vmem(held[rel][0]) for rel in (0, 1)}
    spans = {rel: in_vmem(held[rel][1]) for rel in (0, 1)}
    near = [rel for rel in range(n_tok) if rel < 2]
    far = [rel for rel in range(n_tok) if rel >= 2]

    def key_scratch(rels):
        keys = len(rels) * (cache_rows + tokens)
        return [
            pltpu.VMEM((KD, keys), bf16),
            pltpu.VMEM((keys, KVL), bf16),
            pltpu.VMEM((tokens, keys), f32),
        ]

    group = math.gcd(heads, 4)
    anywhere = pl.BlockSpec(memory_space=pltpu.HBM)
    q = in_vmem(
        pl.pallas_call(
            functools.partial(query_kernel, tokens, group),
            in_specs=[anywhere] * 3,
            out_specs=vmem,
            out_shape=pltpu.VMEM((CHUNKS, heads, rows, KD), bf16),
            scratch_shapes=[
                pltpu.VMEM(q_nope.shape, bf16),
                pltpu.VMEM(q_rope.shape, bf16),
                pltpu.VMEM(w_uk.shape, bf16),
                pltpu.SemaphoreType.DMA((heads // group, 3)),
            ],
            compiler_params=params,
            name="query_latent",
            cost_estimate=cost(2 * tokens * w_uk.size),
        )(*[pltpu.with_memory_space_constraint(x, pltpu.HBM) for x in (q_nope, q_rope, w_uk)])
    )
    group = math.gcd(heads, 8)
    acc, ml = pl.pallas_call(
        functools.partial(local_kernel, near, tokens, group),
        in_specs=[smem] + [vmem] * (1 + 2 * len(near)),
        out_specs=[vmem] * 2,
        out_shape=[
            pltpu.VMEM((CHUNKS, heads, rows, KVL), f32),
            pltpu.VMEM((CHUNKS, heads, rows, 128), f32),
        ],
        scratch_shapes=key_scratch(near),
        compiler_params=params,
        name="local_keys",
        cost_estimate=cost(4 * tokens * heads * len(near) * (cache_rows + tokens) * KD),
    )(prefix_length, q, *[caches[r] for r in near], *[spans[r] for r in near])
    acc, ml = in_vmem(acc), in_vmem(ml)
    others = {rel: both for rel, both in held.items() if rel > 1}
    others, acc, ml = lax.optimization_barrier((others, acc, ml))
    others.update(key_step(others, 1))
    caches.update({rel: in_vmem(both[0]) for rel, both in others.items()})
    spans.update({rel: in_vmem(both[1]) for rel, both in others.items()})
    acc, ml = in_vmem(acc), in_vmem(ml)

    def rest(which):
        return pl.pallas_call(
            functools.partial(rest_kernel, far, tokens, group, which),
            in_specs=[smem] + [vmem] * (4 + 2 * len(far)),
            out_specs=vmem,
            out_shape=pltpu.VMEM((rows, heads * DV), bf16),
            scratch_shapes=key_scratch(far),
            compiler_params=params,
            name="far_keys",
            cost_estimate=cost(4 * rows * heads * len(far) * (cache_rows + tokens) * KD),
        )(prefix_length, q, acc, ml, in_vmem(w_uv), *[caches[r] for r in far], *[spans[r] for r in far])

    columns = w_o.shape[1]
    depth = w_o.shape[0]
    tile = 256 if columns % 256 == 0 else columns
    tiles = columns // tile
    low = bits_of(n_head)
    first = max(1, int(tiles * FIRST))
    groups = [(low, 0, first, tile)]
    if first < tiles:
        groups.append((low[1:] + low[:1], first, tiles - first, tile))

    def project(values):
        half = n_head // 2 * (rows // per)
        return pl.pallas_call(
            functools.partial(project_kernel, n_tok, per, groups),
            in_specs=[vmem] * (n_tok + 1),
            out_specs=[vmem] * (2 * len(groups)),
            out_shape=[
                pltpu.VMEM((half, tile * count), bf16) for _, _, count, _ in groups for _ in "sk"
            ],
            scratch_shapes=[pltpu.VMEM((2 * half, depth), bf16)],
            compiler_params=params,
            name="project",
            cost_estimate=cost(4 * half * depth * columns),
        )(*values, in_vmem(w_o))

    def scatter(send, keep, bits):
        for at, bit in enumerate(bits):
            got = xor_permute(send, "head", bit)
            if at == len(bits) - 1:
                return keep.astype(f32) + got.astype(f32)
            half = keep.shape[0] // 2
            send = (keep[:half].astype(f32) + got[:half].astype(f32)).astype(bf16)
            keep = (keep[half:].astype(f32) + got[half:].astype(f32)).astype(bf16)

    out = []
    for which in range(CHUNKS):
        parts = project(gather(rest(which)))
        out.append(
            jnp.concatenate(
                [
                    scatter(parts[2 * j], parts[2 * j + 1], bits).astype(bf16)
                    for j, (bits, _, _, _) in enumerate(groups)
                ],
                1,
            )
        )
    return jnp.concatenate(out, 0)


def solution(mesh):
    return jax.shard_map(
        shards,
        mesh=mesh,
        in_specs=(
            P("tok", "head"),
            P("tok", "head"),
            P("tok", None),
            P("tok", None),
            P(None, "head"),
            P(None, "head"),
            P("head", "tok"),
            P(),
        ),
        out_specs=P("head", "tok"),
        check_vma=False,
    )
```

```python
import functools
import math

import jax
import jax.numpy as jnp
from jax import lax
from jax.experimental import pallas as pl
from jax.experimental.pallas import tpu as pltpu
from jax.sharding import PartitionSpec as P

DN = 128
DR = 64
DV = 128
KVL = 512
KD = KVL + DR
LANES = 128
KQ = KD + LANES - KD % LANES

MASKED = -1e30
CHUNKS = 2
PLAN = (
    (0.57, lambda bits: [(b,) for b in bits]),
    (0.43, lambda bits: [(b,) for b in bits[1:] + bits[:1]]),
)
COST_SHARE = 1
VMEM_LIMIT = 24 * 1024 * 1024
EXP_SCALE = math.log2(math.e) / math.sqrt(DN + DR)

f32 = jnp.float32
bf16 = jnp.bfloat16


def dot(a, b):
    return jnp.dot(a, b, preferred_element_type=f32)


def dot_t(a, b):
    return lax.dot_general(a, b, (((1,), (1,)), ((), ())), preferred_element_type=f32)


def xor_permute(x, axis, bit):
    n = lax.axis_size(axis)
    return lax.ppermute(x, axis, [(i, i ^ bit) for i in range(n)])


def bits_of(n):
    return [1 << i for i in range(n.bit_length() - 1)]


def in_vmem(x):
    return pltpu.with_memory_space_constraint(x, pltpu.VMEM)


def load_keys(caches, spans, rels, limit, tokens, kt, k):
    me = lax.axis_index("tok")
    cached = caches[0].shape[1]
    size = cached + tokens
    tail = KQ - KD
    first = lax.broadcasted_iota(jnp.int32, (tail, 1), 0) == 0

    def mask(dead):
        return jnp.where(first & dead, MASKED, 0.0).astype(bf16)

    for at, (cache, span, rel) in enumerate(zip(caches, spans, rels)):
        owner = me ^ rel
        start, middle, end = at * size, at * size + cached, (at + 1) * size
        kt[:KD, start:middle] = cache[...]
        kt[:KD, middle:end] = span[...]
        column = lax.broadcasted_iota(jnp.int32, (tail, cached), 1)
        kt[KD:, start:middle] = mask(owner * cached + column >= limit)
        column = lax.broadcasted_iota(jnp.int32, (tail, tokens), 1)
        kt[KD:, middle:end] = mask(owner * tokens + 0 * column > me * tokens)
    k[...] = kt[:KVL, :].T


def lanes(x):
    return [x[:, j : j + LANES] for j in range(0, x.shape[1], LANES)]


def pipelined(count, scores, finish):
    ahead = scores(0)
    for i in range(count):
        now, ahead = ahead, scores(i + 1) if i + 1 < count else None
        finish(i, now)


def softmax(s, top):
    tiles = lanes(s)
    most = functools.reduce(jnp.maximum, tiles)
    new = jnp.broadcast_to(jnp.max(most, axis=1, keepdims=True), most.shape)
    if top is not None:
        new = jnp.maximum(top, new)
    p = [jnp.exp2((x - new) * EXP_SCALE) for x in tiles]
    total = jnp.sum(functools.reduce(jnp.add, p), axis=1, keepdims=True)
    return jnp.concatenate([x.astype(bf16) for x in p], 1), total, new


def split_refs(refs, *counts):
    out, at = [], 0
    for count in counts:
        out.append(refs[at : at + count])
        at += count
    return out + [refs[at:]]


def query_kernel(tokens, group, qn, qr, wuk, q_out, nope, rotary, up, sems):
    half = tokens // 2
    part = half // CHUNKS
    rows = tokens // CHUNKS
    steps = q_out.shape[1] // group

    def copies(i):
        wide = pl.ds(pl.multiple_of(i * group * DN, group * DN), group * DN)
        narrow = pl.ds(pl.multiple_of(i * group * DR, group * DR), group * DR)
        return [
            pltpu.make_async_copy(src.at[:, at], dst.at[:, at], sems.at[i, j])
            for j, (src, dst, at) in enumerate(
                ((wuk, up, wide), (qn, nope, wide), (qr, rotary, narrow))
            )
        ]

    for i in range(steps):
        for copy in copies(i):
            copy.start()

    def ordered(x):
        return jnp.concatenate(
            [
                x[b * half + c * part : b * half + (c + 1) * part]
                for c in range(CHUNKS)
                for b in range(2)
            ],
            0,
        )

    lane = lax.broadcasted_iota(jnp.int32, (rows, KQ - KD), 1)
    ones = jnp.where(lane == 0, 1.0, 0.0).astype(bf16)

    def step(i, _):
        for copy in copies(i):
            copy.wait()
        wide = pl.ds(pl.multiple_of(i * group * DN, group * DN), group * DN)
        narrow = pl.ds(pl.multiple_of(i * group * DR, group * DR), group * DR)
        n, r, w = nope[:, wide], rotary[:, narrow], up[:, wide]
        for g in range(group):
            latent = dot_t(n[:, g * DN : (g + 1) * DN], w[:, g * DN : (g + 1) * DN])
            latent = ordered(latent.astype(bf16))
            rope = ordered(r[:, g * DR : (g + 1) * DR])
            for c in range(CHUNKS):
                q_out[c, i * group + g, :, :KVL] = latent[c * rows : (c + 1) * rows]
                q_out[c, i * group + g, :, KVL:KD] = rope[c * rows : (c + 1) * rows]
                q_out[c, i * group + g, :, KD:] = ones
        return 0

    lax.fori_loop(0, steps, step, 0)


def local_kernel(rels, tokens, group, *refs):
    n = len(rels)
    (limit, q), caches, spans, (acc_out, top_out, sum_out), (kt, k) = split_refs(refs, 2, n, n, 3)
    load_keys(caches, spans, rels, limit[0], tokens, kt, k)
    half = tokens // 2
    part = half // CHUNKS
    rows = tokens // CHUNKS
    steps = q.shape[1] // group
    cached = caches[0].shape[1]
    own = range(cached, cached + tokens)
    row = lax.broadcasted_iota(jnp.int32, (rows, tokens), 0)
    column = lax.broadcasted_iota(jnp.int32, (rows, tokens), 1)

    def place(i):
        return i // steps, slice(i % steps * group, (i % steps + 1) * group)

    def scores(i):
        c, heads = place(i)
        return dot(q[c, heads].reshape(group * rows, KQ), kt[...])

    def finish(i, s):
        c, heads = place(i)
        token = (row // part) * half + c * part + row % part
        later = jnp.where(column > token, MASKED, 0.0)
        here = s[:, own.start : own.stop].reshape(group, rows, tokens) + later[None]
        s = jnp.concatenate(
            [s[:, : own.start], here.reshape(group * rows, tokens), s[:, own.stop :]], 1
        )
        p, total, top = softmax(s, None)
        acc_out[c, heads] = dot(p, k[...]).reshape(group, rows, KVL)
        top_out[c, heads] = top.reshape(group, rows, LANES)
        sum_out[c, heads] = jnp.broadcast_to(total, top.shape).reshape(group, rows, LANES)

    pipelined(CHUNKS * steps, scores, finish)


def rest_kernel(rels, tokens, group, which, *refs):
    n = len(rels)
    (limit, q, acc, top_in, sum_in, wuv), caches, spans, (out,), (kt, k) = split_refs(
        refs, 6, n, n, 1
    )
    load_keys(caches, spans, rels, limit[0], tokens, kt, k)
    rows = tokens // CHUNKS

    def place(i):
        return slice(i * group, (i + 1) * group)

    def scores(i):
        return dot(q[which, place(i)].reshape(group * rows, KQ), kt[...])

    def finish(i, s):
        old = top_in[which, place(i)].reshape(group * rows, LANES)
        p, total, top = softmax(s, old)
        fade = jnp.exp2((old - top) * EXP_SCALE)
        share = 1.0 / (sum_in[which, place(i)].reshape(group * rows, LANES) * fade + total)
        fade = fade * share
        before = lanes(acc[which, place(i)].reshape(group * rows, KVL))
        after = lanes(dot(p, k[...]))
        o = jnp.concatenate(
            [(x * fade + y * share).astype(bf16) for x, y in zip(before, after)], 1
        )
        for g in range(group):
            at = slice((i * group + g) * DV, (i * group + g + 1) * DV)
            out[:, at] = dot(o[g * rows : (g + 1) * rows], wuv[:, at]).astype(bf16)

    pipelined(q.shape[1] // group, scores, finish)


def combinations(bits):
    found = [0]
    for bit in bits:
        found = [x | bit for x in found] + found
    return sorted(found, reverse=True)


def block_order(stages):
    if not stages:
        return [0]
    rest = block_order(stages[1:])
    return [x | r for x in combinations(stages[0]) for r in rest]


def project_kernel(n_tok, per, groups, *refs):
    counts = [len(combinations(stages[0])) for stages, _, _, _ in groups]
    pieces, (w_o,), outs, (lhs,) = split_refs(refs, n_tok, 1, sum(counts))
    part = pieces[0].shape[0] // per
    n = n_tok * per
    me_tok, me_head = lax.axis_index("tok"), lax.axis_index("head")
    for i in range(n_tok):
        for b in range(per):
            rel = ((me_tok ^ i) * per + b) ^ me_head
            start = pl.multiple_of(rel * part, part)
            lhs[pl.ds(start, part), :] = pieces[i][b * part : (b + 1) * part, :]
    for stages, start, count, tile in groups:
        order = block_order(stages)
        ways = len(combinations(stages[0]))
        mine, outs = outs[:ways], outs[ways:]
        rows = n * part // ways
        for t in range(count):
            columns = slice((start + t) * tile, (start + t + 1) * tile)
            here = slice(t * tile, (t + 1) * tile)
            y = dot(lhs[...], w_o[:, columns]).astype(bf16)
            y = jnp.concatenate([y[r * part : (r + 1) * part] for r in order], 0)
            for j, out in enumerate(mine):
                out[:, here] = y[j * rows : (j + 1) * rows]


def shards(q_nope, q_rope, cache_kv, span_kv, w_uk, w_uv, w_o, prefix_length):
    tokens = q_nope.shape[0]
    heads = w_uk.shape[1] // DN
    cache_rows = cache_kv.shape[0]
    n_tok, n_head = lax.axis_size("tok"), lax.axis_size("head")
    per = n_head // n_tok
    rows = tokens // CHUNKS
    params = pltpu.CompilerParams(vmem_limit_bytes=VMEM_LIMIT)
    smem = pl.BlockSpec(memory_space=pltpu.SMEM)
    vmem = pl.BlockSpec(memory_space=pltpu.VMEM)

    def step(held, axis_bit):
        return {rel ^ axis_bit: xor_permute(v, "tok", axis_bit) for rel, v in held.items()}

    def gather(x):
        held = {0: x}
        for bit in reversed(bits_of(n_tok)):
            held.update(step(held, bit))
        return [in_vmem(held[rel]) for rel in range(n_tok)]

    def cost(flops):
        return pl.CostEstimate(flops=flops // COST_SHARE, bytes_accessed=0, transcendentals=0)

    held = {0: (cache_kv.T, span_kv.T)}

    def key_step(held, bit):
        return {
            rel ^ bit: tuple(xor_permute(v, "tok", bit) for v in both)
            for rel, both in held.items()
        }

    for bit in reversed(bits_of(n_tok)[1:]):
        held.update(key_step(held, bit))
    held.update(key_step({0: held[0]}, 1))
    caches = {rel: in_vmem(held[rel][0]) for rel in (0, 1)}
    spans = {rel: in_vmem(held[rel][1]) for rel in (0, 1)}
    near = [rel for rel in range(n_tok) if rel < 2]
    far = [rel for rel in range(n_tok) if rel >= 2]

    def key_scratch(rels):
        keys = len(rels) * (cache_rows + tokens)
        return [
            pltpu.VMEM((KQ, keys), bf16),
            pltpu.VMEM((keys, KVL), bf16),
        ]

    group = math.gcd(heads, 4)
    anywhere = pl.BlockSpec(memory_space=pltpu.HBM)
    q = in_vmem(
        pl.pallas_call(
            functools.partial(query_kernel, tokens, group),
            in_specs=[anywhere] * 3,
            out_specs=vmem,
            out_shape=pltpu.VMEM((CHUNKS, heads, rows, KQ), bf16),
            scratch_shapes=[
                pltpu.VMEM(q_nope.shape, bf16),
                pltpu.VMEM(q_rope.shape, bf16),
                pltpu.VMEM(w_uk.shape, bf16),
                pltpu.SemaphoreType.DMA((heads // group, 3)),
            ],
            compiler_params=params,
            name="query_latent",
            cost_estimate=cost(2 * tokens * w_uk.size),
        )(*[pltpu.with_memory_space_constraint(x, pltpu.HBM) for x in (q_nope, q_rope, w_uk)])
    )
    group = math.gcd(heads, 8)
    state = pl.pallas_call(
        functools.partial(local_kernel, near, tokens, group),
        in_specs=[smem] + [vmem] * (1 + 2 * len(near)),
        out_specs=[vmem] * 3,
        out_shape=[
            pltpu.VMEM((CHUNKS, heads, rows, KVL), f32),
            pltpu.VMEM((CHUNKS, heads, rows, LANES), f32),
            pltpu.VMEM((CHUNKS, heads, rows, LANES), f32),
        ],
        scratch_shapes=key_scratch(near),
        compiler_params=params,
        name="local_keys",
        cost_estimate=cost(4 * tokens * heads * len(near) * (cache_rows + tokens) * KD),
    )(prefix_length, q, *[caches[r] for r in near], *[spans[r] for r in near])
    others = {rel: both for rel, both in held.items() if rel > 1}
    others, state = lax.optimization_barrier((others, state))
    others.update(key_step(others, 1))
    caches.update({rel: in_vmem(both[0]) for rel, both in others.items()})
    spans.update({rel: in_vmem(both[1]) for rel, both in others.items()})
    state = [in_vmem(x) for x in state]

    def rest(which):
        return pl.pallas_call(
            functools.partial(rest_kernel, far, tokens, group, which),
            in_specs=[smem] + [vmem] * (5 + 2 * len(far)),
            out_specs=vmem,
            out_shape=pltpu.VMEM((rows, heads * DV), bf16),
            scratch_shapes=key_scratch(far),
            compiler_params=params,
            name="far_keys",
            cost_estimate=cost(4 * rows * heads * len(far) * (cache_rows + tokens) * KD),
        )(prefix_length, q, *state, in_vmem(w_uv), *[caches[r] for r in far], *[spans[r] for r in far])

    columns = w_o.shape[1]
    depth = w_o.shape[0]
    tile = 256 if columns % 256 == 0 else columns
    tiles = columns // tile
    groups, start = [], 0
    for at, (share, stages) in enumerate(PLAN):
        count = round(tiles * share)
        if at == len(PLAN) - 1:
            count = tiles - start
        if count > 0:
            groups.append((stages(bits_of(n_head)), start, count, tile))
            start += count

    def project(values):
        shapes = [
            pltpu.VMEM((n_head // ways * (rows // per), tile * count), bf16)
            for ways, count in (
                (len(combinations(stages[0])), count) for stages, _, count, _ in groups
            )
            for _ in range(ways)
        ]
        return pl.pallas_call(
            functools.partial(project_kernel, n_tok, per, groups),
            in_specs=[vmem] * (n_tok + 1),
            out_specs=[vmem] * len(shapes),
            out_shape=shapes,
            scratch_shapes=[pltpu.VMEM((n_head // per * rows, depth), bf16)],
            compiler_params=params,
            name="project",
            cost_estimate=cost(2 * n_head // per * rows * depth * columns),
        )(*values, in_vmem(w_o))

    def scatter(parts, stages):
        for at, bits in enumerate(stages):
            moves = combinations(bits)[:-1]
            got = [xor_permute(x, "head", move) for x, move in zip(parts, moves)]
            terms = [parts[-1]] + got
            ways = len(combinations(stages[at + 1])) if at + 1 < len(stages) else 1
            size = terms[0].shape[0] // ways
            parts = [
                sum(x[j * size : (j + 1) * size].astype(f32) for x in terms).astype(bf16)
                for j in range(ways)
            ]
        return parts[0]

    out = []
    for which in range(CHUNKS):
        parts = list(project(gather(rest(which))))
        ends = []
        for stages, _, _, _ in groups:
            ways = len(combinations(stages[0]))
            ends.append(scatter(parts[:ways], stages))
            parts = parts[ways:]
        out.append(jnp.concatenate(ends, 1))
    return jnp.concatenate(out, 0)


def solution(mesh):
    return jax.shard_map(
        shards,
        mesh=mesh,
        in_specs=(
            P("tok", "head"),
            P("tok", "head"),
            P("tok", None),
            P("tok", None),
            P(None, "head"),
            P(None, "head"),
            P("head", "tok"),
            P(),
        ),
        out_specs=P("head", "tok"),
        check_vma=False,
    )
```

```python
import functools
import math

import jax
import jax.numpy as jnp
from jax import lax
from jax.experimental import pallas as pl
from jax.experimental.pallas import tpu as pltpu
from jax.sharding import PartitionSpec as P

DN = 128
DR = 64
DV = 128
KVL = 512
KD = KVL + DR
LANES = 128
KQ = KD + LANES - KD % LANES

MASKED = -1e30
CHUNKS = 2
PLAN = (
    (0.57, lambda bits: [(b,) for b in bits]),
    (0.43, lambda bits: [(b,) for b in bits[1:] + bits[:1]]),
)
COST_SHARE = 1
AHEAD = 1
VMEM_LIMIT = 24 * 1024 * 1024
EXP_SCALE = math.log2(math.e) / math.sqrt(DN + DR)

f32 = jnp.float32
bf16 = jnp.bfloat16


def dot(a, b):
    return jnp.dot(a, b, preferred_element_type=f32)


def dot_t(a, b):
    return lax.dot_general(a, b, (((1,), (1,)), ((), ())), preferred_element_type=f32)


def xor_permute(x, axis, bit):
    n = lax.axis_size(axis)
    return lax.ppermute(x, axis, [(i, i ^ bit) for i in range(n)])


def bits_of(n):
    return [1 << i for i in range(n.bit_length() - 1)]


def in_vmem(x):
    return pltpu.with_memory_space_constraint(x, pltpu.VMEM)


def load_keys(caches, spans, rels, limit, tokens, kt, k):
    me = lax.axis_index("tok")
    cached = caches[0].shape[1]
    size = cached + tokens
    tail = KQ - KD
    first = lax.broadcasted_iota(jnp.int32, (tail, 1), 0) == 0

    def mask(dead):
        return jnp.where(first & dead, MASKED, 0.0).astype(bf16)

    for at, (cache, span, rel) in enumerate(zip(caches, spans, rels)):
        owner = me ^ rel
        start, middle, end = at * size, at * size + cached, (at + 1) * size
        kt[:KD, start:middle] = cache[...]
        kt[:KD, middle:end] = span[...]
        column = lax.broadcasted_iota(jnp.int32, (tail, cached), 1)
        kt[KD:, start:middle] = mask(owner * cached + column >= limit)
        column = lax.broadcasted_iota(jnp.int32, (tail, tokens), 1)
        kt[KD:, middle:end] = mask(owner * tokens + 0 * column > me * tokens)
    k[...] = kt[:KVL, :].T


def lanes(x):
    return [x[:, j : j + LANES] for j in range(0, x.shape[1], LANES)]


def pipelined(count, scores, finish):
    ahead = scores(0)
    for i in range(count):
        now, ahead = ahead, scores(i + 1) if i + 1 < count else None
        finish(i, now)


def softmax(s, top):
    tiles = lanes(s)
    most = functools.reduce(jnp.maximum, tiles)
    new = jnp.broadcast_to(jnp.max(most, axis=1, keepdims=True), most.shape)
    if top is not None:
        new = jnp.maximum(top, new)
    p = [jnp.exp2((x - new) * EXP_SCALE) for x in tiles]
    total = jnp.sum(functools.reduce(jnp.add, p), axis=1, keepdims=True)
    return jnp.concatenate([x.astype(bf16) for x in p], 1), total, new


def split_refs(refs, *counts):
    out, at = [], 0
    for count in counts:
        out.append(refs[at : at + count])
        at += count
    return out + [refs[at:]]


def query_kernel(tokens, group, qn, qr, wuk, q_out, nope, rotary, up, sems):
    half = tokens // 2
    part = half // CHUNKS
    rows = tokens // CHUNKS
    steps = q_out.shape[1] // group

    def copies(i):
        wide = pl.ds(pl.multiple_of(i * group * DN, group * DN), group * DN)
        narrow = pl.ds(pl.multiple_of(i * group * DR, group * DR), group * DR)
        return [
            pltpu.make_async_copy(src.at[:, at], dst.at[:, at], sems.at[i, j])
            for j, (src, dst, at) in enumerate(
                ((wuk, up, wide), (qn, nope, wide), (qr, rotary, narrow))
            )
        ]

    for i in range(steps):
        for copy in copies(i):
            copy.start()

    def ordered(x):
        return jnp.concatenate(
            [
                x[b * half + c * part : b * half + (c + 1) * part]
                for c in range(CHUNKS)
                for b in range(2)
            ],
            0,
        )

    lane = lax.broadcasted_iota(jnp.int32, (rows, KQ - KD), 1)
    ones = jnp.where(lane == 0, 1.0, 0.0).astype(bf16)

    def step(i, _):
        for copy in copies(i):
            copy.wait()
        wide = pl.ds(pl.multiple_of(i * group * DN, group * DN), group * DN)
        narrow = pl.ds(pl.multiple_of(i * group * DR, group * DR), group * DR)
        n, r, w = nope[:, wide], rotary[:, narrow], up[:, wide]
        for g in range(group):
            latent = dot_t(n[:, g * DN : (g + 1) * DN], w[:, g * DN : (g + 1) * DN])
            latent = ordered(latent.astype(bf16))
            rope = ordered(r[:, g * DR : (g + 1) * DR])
            for c in range(CHUNKS):
                q_out[c, i * group + g, :, :KVL] = latent[c * rows : (c + 1) * rows]
                q_out[c, i * group + g, :, KVL:KD] = rope[c * rows : (c + 1) * rows]
                q_out[c, i * group + g, :, KD:] = ones
        return 0

    lax.fori_loop(0, steps, step, 0)


def local_kernel(rels, tokens, group, *refs):
    n = len(rels)
    (limit, q), caches, spans, (acc_out, top_out, sum_out), (kt, k) = split_refs(refs, 2, n, n, 3)
    load_keys(caches, spans, rels, limit[0], tokens, kt, k)
    half = tokens // 2
    part = half // CHUNKS
    rows = tokens // CHUNKS
    steps = q.shape[1] // group
    cached = caches[0].shape[1]
    own = range(cached, cached + tokens)
    row = lax.broadcasted_iota(jnp.int32, (rows, tokens), 0)
    column = lax.broadcasted_iota(jnp.int32, (rows, tokens), 1)

    def place(i):
        return i // steps, slice(i % steps * group, (i % steps + 1) * group)

    def scores(i):
        c, heads = place(i)
        return dot(q[c, heads].reshape(group * rows, KQ), kt[...])

    def finish(i, s):
        c, heads = place(i)
        token = (row // part) * half + c * part + row % part
        later = jnp.where(column > token, MASKED, 0.0)
        here = s[:, own.start : own.stop].reshape(group, rows, tokens) + later[None]
        s = jnp.concatenate(
            [s[:, : own.start], here.reshape(group * rows, tokens), s[:, own.stop :]], 1
        )
        p, total, top = softmax(s, None)
        acc_out[c, heads] = dot(p, k[...]).reshape(group, rows, KVL)
        top_out[c, heads] = top.reshape(group, rows, LANES)
        sum_out[c, heads] = jnp.broadcast_to(total, top.shape).reshape(group, rows, LANES)

    pipelined(CHUNKS * steps, scores, finish)


def step_kernel(rels, tokens, group, which, last, *refs):
    n = len(rels)
    (limit, q, acc, top_in, sum_in, *up), caches, spans, outs, (kt, k) = split_refs(
        refs, 6 if last else 5, n, n, 1 if last else 3
    )
    load_keys(caches, spans, rels, limit[0], tokens, kt, k)
    rows = tokens // CHUNKS
    at_state = which if acc.shape[0] == CHUNKS else 0

    def place(i):
        return slice(i * group, (i + 1) * group)

    def scores(i):
        return dot(q[which, place(i)].reshape(group * rows, KQ), kt[...])

    def finish(i, s):
        old = top_in[at_state, place(i)].reshape(group * rows, LANES)
        p, total, top = softmax(s, old)
        fade = jnp.exp2((old - top) * EXP_SCALE)
        total = sum_in[at_state, place(i)].reshape(group * rows, LANES) * fade + total
        before = lanes(acc[at_state, place(i)].reshape(group * rows, KVL))
        after = lanes(dot(p, k[...]))
        if not last:
            acc_out, top_out, sum_out = outs
            o = jnp.concatenate([x * fade + y for x, y in zip(before, after)], 1)
            acc_out[0, place(i)] = o.reshape(group, rows, KVL)
            top_out[0, place(i)] = top.reshape(group, rows, LANES)
            sum_out[0, place(i)] = total.reshape(group, rows, LANES)
            return
        share = 1.0 / total
        fade = fade * share
        o = jnp.concatenate(
            [(x * fade + y * share).astype(bf16) for x, y in zip(before, after)], 1
        )
        for g in range(group):
            at = slice((i * group + g) * DV, (i * group + g + 1) * DV)
            outs[0][:, at] = dot(o[g * rows : (g + 1) * rows], up[0][:, at]).astype(bf16)

    pipelined(q.shape[1] // group, scores, finish)


def combinations(bits):
    found = [0]
    for bit in bits:
        found = [x | bit for x in found] + found
    return sorted(found, reverse=True)


def block_order(stages):
    if not stages:
        return [0]
    rest = block_order(stages[1:])
    return [x | r for x in combinations(stages[0]) for r in rest]


def project_kernel(n_tok, per, groups, *refs):
    counts = [len(combinations(stages[0])) for stages, _, _, _ in groups]
    pieces, (w_o,), outs, (lhs,) = split_refs(refs, n_tok, 1, sum(counts))
    part = pieces[0].shape[0] // per
    n = n_tok * per
    me_tok, me_head = lax.axis_index("tok"), lax.axis_index("head")
    for i in range(n_tok):
        for b in range(per):
            rel = ((me_tok ^ i) * per + b) ^ me_head
            start = pl.multiple_of(rel * part, part)
            lhs[pl.ds(start, part), :] = pieces[i][b * part : (b + 1) * part, :]
    for stages, start, count, tile in groups:
        order = block_order(stages)
        ways = len(combinations(stages[0]))
        mine, outs = outs[:ways], outs[ways:]
        rows = n * part // ways
        for t in range(count):
            columns = slice((start + t) * tile, (start + t + 1) * tile)
            here = slice(t * tile, (t + 1) * tile)
            y = dot(lhs[...], w_o[:, columns]).astype(bf16)
            y = jnp.concatenate([y[r * part : (r + 1) * part] for r in order], 0)
            for j, out in enumerate(mine):
                out[:, here] = y[j * rows : (j + 1) * rows]


def shards(q_nope, q_rope, cache_kv, span_kv, w_uk, w_uv, w_o, prefix_length):
    tokens = q_nope.shape[0]
    heads = w_uk.shape[1] // DN
    cache_rows = cache_kv.shape[0]
    n_tok, n_head = lax.axis_size("tok"), lax.axis_size("head")
    per = n_head // n_tok
    rows = tokens // CHUNKS
    params = pltpu.CompilerParams(vmem_limit_bytes=VMEM_LIMIT)
    smem = pl.BlockSpec(memory_space=pltpu.SMEM)
    vmem = pl.BlockSpec(memory_space=pltpu.VMEM)

    def step(held, axis_bit):
        return {rel ^ axis_bit: xor_permute(v, "tok", axis_bit) for rel, v in held.items()}

    def gather(x):
        held = {0: x}
        for bit in reversed(bits_of(n_tok)):
            held.update(step(held, bit))
        return [in_vmem(held[rel]) for rel in range(n_tok)]

    def cost(flops):
        return pl.CostEstimate(flops=flops // COST_SHARE, bytes_accessed=0, transcendentals=0)

    held = {0: (cache_kv.T, span_kv.T)}

    def key_step(held, bit):
        return {
            rel ^ bit: tuple(xor_permute(v, "tok", bit) for v in both)
            for rel, both in held.items()
        }

    for bit in reversed(bits_of(n_tok)[1:]):
        held.update(key_step(held, bit))
    held.update(key_step({0: held[0]}, 1))
    caches = {rel: in_vmem(held[rel][0]) for rel in (0, 1)}
    spans = {rel: in_vmem(held[rel][1]) for rel in (0, 1)}
    near = [rel for rel in range(n_tok) if rel < 2]
    far = [rel for rel in range(n_tok) if rel >= 2]

    def key_scratch(rels):
        keys = len(rels) * (cache_rows + tokens)
        return [
            pltpu.VMEM((KQ, keys), bf16),
            pltpu.VMEM((keys, KVL), bf16),
        ]

    group = math.gcd(heads, 4)
    anywhere = pl.BlockSpec(memory_space=pltpu.HBM)
    q = in_vmem(
        pl.pallas_call(
            functools.partial(query_kernel, tokens, group),
            in_specs=[anywhere] * 3,
            out_specs=vmem,
            out_shape=pltpu.VMEM((CHUNKS, heads, rows, KQ), bf16),
            scratch_shapes=[
                pltpu.VMEM(q_nope.shape, bf16),
                pltpu.VMEM(q_rope.shape, bf16),
                pltpu.VMEM(w_uk.shape, bf16),
                pltpu.SemaphoreType.DMA((heads // group, 3)),
            ],
            compiler_params=params,
            name="query_latent",
            cost_estimate=cost(2 * tokens * w_uk.size),
        )(*[pltpu.with_memory_space_constraint(x, pltpu.HBM) for x in (q_nope, q_rope, w_uk)])
    )
    group = math.gcd(heads, 8)
    state = pl.pallas_call(
        functools.partial(local_kernel, near, tokens, group),
        in_specs=[smem] + [vmem] * (1 + 2 * len(near)),
        out_specs=[vmem] * 3,
        out_shape=[
            pltpu.VMEM((CHUNKS, heads, rows, KVL), f32),
            pltpu.VMEM((CHUNKS, heads, rows, LANES), f32),
            pltpu.VMEM((CHUNKS, heads, rows, LANES), f32),
        ],
        scratch_shapes=key_scratch(near),
        compiler_params=params,
        name="local_keys",
        cost_estimate=cost(4 * tokens * heads * len(near) * (cache_rows + tokens) * KD),
    )(prefix_length, q, *[caches[r] for r in near], *[spans[r] for r in near])
    others = {rel: both for rel, both in held.items() if rel > 1}
    others, state = lax.optimization_barrier((others, state))
    caches.update({rel: in_vmem(both[0]) for rel, both in others.items()})
    spans.update({rel: in_vmem(both[1]) for rel, both in others.items()})

    def go_on(which, rels, state, last):
        if last:
            shapes = [pltpu.VMEM((rows, heads * DV), bf16)]
        else:
            shapes = [
                pltpu.VMEM((1, heads, rows, KVL), f32),
                pltpu.VMEM((1, heads, rows, LANES), f32),
                pltpu.VMEM((1, heads, rows, LANES), f32),
            ]
        up = [in_vmem(w_uv)] if last else []
        return pl.pallas_call(
            functools.partial(step_kernel, rels, tokens, group, which, last),
            in_specs=[smem] + [vmem] * (4 + len(up) + 2 * len(rels)),
            out_specs=[vmem] * len(shapes),
            out_shape=shapes,
            scratch_shapes=key_scratch(rels),
            compiler_params=params,
            name="far_keys" if last else "counterpart_keys",
            cost_estimate=cost(4 * rows * heads * len(rels) * (cache_rows + tokens) * KD),
        )(
            prefix_length,
            q,
            *[in_vmem(x) for x in state],
            *up,
            *[caches[r] for r in rels],
            *[spans[r] for r in rels],
        )

    straight = [go_on(which, [r for r in far if r % 2 == 0], state, False) for which in range(AHEAD)]
    crossed = key_step(others, 1)
    if AHEAD:
        crossed, straight = lax.optimization_barrier((crossed, straight))
    caches.update({rel: in_vmem(both[0]) for rel, both in crossed.items()})
    spans.update({rel: in_vmem(both[1]) for rel, both in crossed.items()})

    def rest(which):
        if which < AHEAD:
            return go_on(which, [rel for rel in far if rel % 2], straight[which], True)[0]
        return go_on(which, far, state, True)[0]

    columns = w_o.shape[1]
    depth = w_o.shape[0]
    tile = 256 if columns % 256 == 0 else columns
    tiles = columns // tile
    groups, start = [], 0
    for at, (share, stages) in enumerate(PLAN):
        count = round(tiles * share)
        if at == len(PLAN) - 1:
            count = tiles - start
        if count > 0:
            groups.append((stages(bits_of(n_head)), start, count, tile))
            start += count

    def project(values):
        shapes = [
            pltpu.VMEM((n_head // ways * (rows // per), tile * count), bf16)
            for ways, count in (
                (len(combinations(stages[0])), count) for stages, _, count, _ in groups
            )
            for _ in range(ways)
        ]
        return pl.pallas_call(
            functools.partial(project_kernel, n_tok, per, groups),
            in_specs=[vmem] * (n_tok + 1),
            out_specs=[vmem] * len(shapes),
            out_shape=shapes,
            scratch_shapes=[pltpu.VMEM((n_head // per * rows, depth), bf16)],
            compiler_params=params,
            name="project",
            cost_estimate=cost(2 * n_head // per * rows * depth * columns),
        )(*values, in_vmem(w_o))

    def scatter(parts, stages):
        for at, bits in enumerate(stages):
            moves = combinations(bits)[:-1]
            got = [xor_permute(x, "head", move) for x, move in zip(parts, moves)]
            terms = [parts[-1]] + got
            ways = len(combinations(stages[at + 1])) if at + 1 < len(stages) else 1
            size = terms[0].shape[0] // ways
            parts = [
                sum(x[j * size : (j + 1) * size].astype(f32) for x in terms).astype(bf16)
                for j in range(ways)
            ]
        return parts[0]

    out = []
    for which in range(CHUNKS):
        parts = list(project(gather(rest(which))))
        ends = []
        for stages, _, _, _ in groups:
            ways = len(combinations(stages[0]))
            ends.append(scatter(parts[:ways], stages))
            parts = parts[ways:]
        out.append(jnp.concatenate(ends, 1))
    return jnp.concatenate(out, 0)


def solution(mesh):
    return jax.shard_map(
        shards,
        mesh=mesh,
        in_specs=(
            P("tok", "head"),
            P("tok", "head"),
            P("tok", None),
            P("tok", None),
            P(None, "head"),
            P(None, "head"),
            P("head", "tok"),
            P(),
        ),
        out_specs=P("head", "tok"),
        check_vma=False,
    )
```

```python
import functools
import math

import jax
import jax.numpy as jnp
from jax import lax
from jax.experimental import pallas as pl
from jax.experimental.pallas import tpu as pltpu
from jax.sharding import PartitionSpec as P

DN = 128
DR = 64
DV = 128
KVL = 512
KD = KVL + DR
LANES = 128
KQ = KD + LANES - KD % LANES

MASKED = -1e30
CHUNKS = 2
PLAN = (
    (0.57, lambda bits: [(b,) for b in bits]),
    (0.43, lambda bits: [(b,) for b in bits[1:] + bits[:1]]),
)
COST_SHARE = 1
AHEAD = 2
VMEM_LIMIT = 24 * 1024 * 1024
EXP_SCALE = math.log2(math.e) / math.sqrt(DN + DR)

f32 = jnp.float32
bf16 = jnp.bfloat16


def dot(a, b):
    return jnp.dot(a, b, preferred_element_type=f32)


def dot_t(a, b):
    return lax.dot_general(a, b, (((1,), (1,)), ((), ())), preferred_element_type=f32)


def xor_permute(x, axis, bit):
    n = lax.axis_size(axis)
    return lax.ppermute(x, axis, [(i, i ^ bit) for i in range(n)])


def bits_of(n):
    return [1 << i for i in range(n.bit_length() - 1)]


def in_vmem(x):
    return pltpu.with_memory_space_constraint(x, pltpu.VMEM)


def load_keys(caches, spans, rels, limit, tokens, kt, k):
    me = lax.axis_index("tok")
    cached = caches[0].shape[1]
    size = cached + tokens
    tail = KQ - KD
    first = lax.broadcasted_iota(jnp.int32, (tail, 1), 0) == 0

    def mask(dead):
        return jnp.where(first & dead, MASKED, 0.0).astype(bf16)

    for at, (cache, span, rel) in enumerate(zip(caches, spans, rels)):
        owner = me ^ rel
        start, middle, end = at * size, at * size + cached, (at + 1) * size
        kt[:KD, start:middle] = cache[...]
        kt[:KD, middle:end] = span[...]
        column = lax.broadcasted_iota(jnp.int32, (tail, cached), 1)
        kt[KD:, start:middle] = mask(owner * cached + column >= limit)
        column = lax.broadcasted_iota(jnp.int32, (tail, tokens), 1)
        kt[KD:, middle:end] = mask(owner * tokens + 0 * column > me * tokens)
    k[...] = kt[:KVL, :].T


def lanes(x):
    return [x[:, j : j + LANES] for j in range(0, x.shape[1], LANES)]


def pipelined(count, scores, finish):
    ahead = scores(0)
    for i in range(count):
        now, ahead = ahead, scores(i + 1) if i + 1 < count else None
        finish(i, now)


def softmax(s, top):
    tiles = lanes(s)
    most = functools.reduce(jnp.maximum, tiles)
    new = jnp.broadcast_to(jnp.max(most, axis=1, keepdims=True), most.shape)
    if top is not None:
        new = jnp.maximum(top, new)
    p = [jnp.exp2((x - new) * EXP_SCALE) for x in tiles]
    total = jnp.sum(functools.reduce(jnp.add, p), axis=1, keepdims=True)
    return jnp.concatenate([x.astype(bf16) for x in p], 1), total, new


def split_refs(refs, *counts):
    out, at = [], 0
    for count in counts:
        out.append(refs[at : at + count])
        at += count
    return out + [refs[at:]]


def query_kernel(tokens, group, qn, qr, wuk, q_out, nope, rotary, up, sems):
    half = tokens // 2
    part = half // CHUNKS
    rows = tokens // CHUNKS
    steps = q_out.shape[1] // group

    def copies(i):
        wide = pl.ds(pl.multiple_of(i * group * DN, group * DN), group * DN)
        narrow = pl.ds(pl.multiple_of(i * group * DR, group * DR), group * DR)
        return [
            pltpu.make_async_copy(src.at[:, at], dst.at[:, at], sems.at[i, j])
            for j, (src, dst, at) in enumerate(
                ((wuk, up, wide), (qn, nope, wide), (qr, rotary, narrow))
            )
        ]

    for i in range(steps):
        for copy in copies(i):
            copy.start()

    def ordered(x):
        return jnp.concatenate(
            [
                x[b * half + c * part : b * half + (c + 1) * part]
                for c in range(CHUNKS)
                for b in range(2)
            ],
            0,
        )

    lane = lax.broadcasted_iota(jnp.int32, (rows, KQ - KD), 1)
    ones = jnp.where(lane == 0, 1.0, 0.0).astype(bf16)

    def step(i, _):
        for copy in copies(i):
            copy.wait()
        wide = pl.ds(pl.multiple_of(i * group * DN, group * DN), group * DN)
        narrow = pl.ds(pl.multiple_of(i * group * DR, group * DR), group * DR)
        n, r, w = nope[:, wide], rotary[:, narrow], up[:, wide]
        for g in range(group):
            latent = dot_t(n[:, g * DN : (g + 1) * DN], w[:, g * DN : (g + 1) * DN])
            latent = ordered(latent.astype(bf16))
            rope = ordered(r[:, g * DR : (g + 1) * DR])
            for c in range(CHUNKS):
                q_out[c, i * group + g, :, :KVL] = latent[c * rows : (c + 1) * rows]
                q_out[c, i * group + g, :, KVL:KD] = rope[c * rows : (c + 1) * rows]
                q_out[c, i * group + g, :, KD:] = ones
        return 0

    lax.fori_loop(0, steps, step, 0)


def local_kernel(rels, tokens, group, *refs):
    n = len(rels)
    (limit, q), caches, spans, (acc_out, top_out, sum_out), (kt, k) = split_refs(refs, 2, n, n, 3)
    load_keys(caches, spans, rels, limit[0], tokens, kt, k)
    half = tokens // 2
    part = half // CHUNKS
    rows = tokens // CHUNKS
    steps = q.shape[1] // group
    cached = caches[0].shape[1]
    own = range(cached, cached + tokens)
    row = lax.broadcasted_iota(jnp.int32, (rows, tokens), 0)
    column = lax.broadcasted_iota(jnp.int32, (rows, tokens), 1)

    def place(i):
        return i // steps, slice(i % steps * group, (i % steps + 1) * group)

    def scores(i):
        c, heads = place(i)
        return dot(q[c, heads].reshape(group * rows, KQ), kt[...])

    def finish(i, s):
        c, heads = place(i)
        token = (row // part) * half + c * part + row % part
        later = jnp.where(column > token, MASKED, 0.0)
        here = s[:, own.start : own.stop].reshape(group, rows, tokens) + later[None]
        s = jnp.concatenate(
            [s[:, : own.start], here.reshape(group * rows, tokens), s[:, own.stop :]], 1
        )
        p, total, top = softmax(s, None)
        acc_out[c, heads] = dot(p, k[...]).reshape(group, rows, KVL)
        top_out[c, heads] = top.reshape(group, rows, LANES)
        sum_out[c, heads] = jnp.broadcast_to(total, top.shape).reshape(group, rows, LANES)

    pipelined(CHUNKS * steps, scores, finish)


def step_kernel(rels, tokens, group, which, last, *refs):
    n = len(rels)
    (limit, q, acc, top_in, sum_in, *up), caches, spans, outs, (kt, k) = split_refs(
        refs, 6 if last else 5, n, n, 1 if last else 3
    )
    load_keys(caches, spans, rels, limit[0], tokens, kt, k)
    rows = tokens // CHUNKS
    at_state = which if acc.shape[0] == CHUNKS else 0

    def place(i):
        return slice(i * group, (i + 1) * group)

    def scores(i):
        return dot(q[which, place(i)].reshape(group * rows, KQ), kt[...])

    def finish(i, s):
        old = top_in[at_state, place(i)].reshape(group * rows, LANES)
        p, total, top = softmax(s, old)
        fade = jnp.exp2((old - top) * EXP_SCALE)
        total = sum_in[at_state, place(i)].reshape(group * rows, LANES) * fade + total
        before = lanes(acc[at_state, place(i)].reshape(group * rows, KVL))
        after = lanes(dot(p, k[...]))
        if not last:
            acc_out, top_out, sum_out = outs
            o = jnp.concatenate([x * fade + y for x, y in zip(before, after)], 1)
            acc_out[0, place(i)] = o.reshape(group, rows, KVL)
            top_out[0, place(i)] = top.reshape(group, rows, LANES)
            sum_out[0, place(i)] = total.reshape(group, rows, LANES)
            return
        share = 1.0 / total
        fade = fade * share
        o = jnp.concatenate(
            [(x * fade + y * share).astype(bf16) for x, y in zip(before, after)], 1
        )
        for g in range(group):
            at = slice((i * group + g) * DV, (i * group + g + 1) * DV)
            outs[0][:, at] = dot(o[g * rows : (g + 1) * rows], up[0][:, at]).astype(bf16)

    pipelined(q.shape[1] // group, scores, finish)


def combinations(bits):
    found = [0]
    for bit in bits:
        found = [x | bit for x in found] + found
    return sorted(found, reverse=True)


def block_order(stages):
    if not stages:
        return [0]
    rest = block_order(stages[1:])
    return [x | r for x in combinations(stages[0]) for r in rest]


def project_kernel(n_tok, per, groups, *refs):
    counts = [len(combinations(stages[0])) for stages, _, _, _ in groups]
    pieces, (w_o,), outs, (lhs,) = split_refs(refs, n_tok, 1, sum(counts))
    part = pieces[0].shape[0] // per
    n = n_tok * per
    me_tok, me_head = lax.axis_index("tok"), lax.axis_index("head")
    for i in range(n_tok):
        for b in range(per):
            rel = ((me_tok ^ i) * per + b) ^ me_head
            start = pl.multiple_of(rel * part, part)
            lhs[pl.ds(start, part), :] = pieces[i][b * part : (b + 1) * part, :]
    for stages, start, count, tile in groups:
        order = block_order(stages)
        ways = len(combinations(stages[0]))
        mine, outs = outs[:ways], outs[ways:]
        rows = n * part // ways
        for t in range(count):
            columns = slice((start + t) * tile, (start + t + 1) * tile)
            here = slice(t * tile, (t + 1) * tile)
            y = dot(lhs[...], w_o[:, columns]).astype(bf16)
            y = jnp.concatenate([y[r * part : (r + 1) * part] for r in order], 0)
            for j, out in enumerate(mine):
                out[:, here] = y[j * rows : (j + 1) * rows]


def join_kernel(places, *refs):
    *terms, out = refs
    for row, column, count in places:
        mine, terms = terms[:count], terms[count:]
        height, width = mine[0].shape
        total = sum(x[...].astype(f32) for x in mine)
        out[row : row + height, column : column + width] = total.astype(bf16)


def shards(q_nope, q_rope, cache_kv, span_kv, w_uk, w_uv, w_o, prefix_length):
    tokens = q_nope.shape[0]
    heads = w_uk.shape[1] // DN
    cache_rows = cache_kv.shape[0]
    n_tok, n_head = lax.axis_size("tok"), lax.axis_size("head")
    per = n_head // n_tok
    rows = tokens // CHUNKS
    params = pltpu.CompilerParams(vmem_limit_bytes=VMEM_LIMIT)
    smem = pl.BlockSpec(memory_space=pltpu.SMEM)
    vmem = pl.BlockSpec(memory_space=pltpu.VMEM)

    def step(held, axis_bit):
        return {rel ^ axis_bit: xor_permute(v, "tok", axis_bit) for rel, v in held.items()}

    def gather(x):
        held = {0: x}
        for bit in reversed(bits_of(n_tok)):
            held.update(step(held, bit))
        return [in_vmem(held[rel]) for rel in range(n_tok)]

    def cost(flops):
        return pl.CostEstimate(flops=flops // COST_SHARE, bytes_accessed=0, transcendentals=0)

    held = {0: (cache_kv.T, span_kv.T)}

    def key_step(held, bit):
        return {
            rel ^ bit: tuple(xor_permute(v, "tok", bit) for v in both)
            for rel, both in held.items()
        }

    for bit in reversed(bits_of(n_tok)[1:]):
        held.update(key_step(held, bit))
    held.update(key_step({0: held[0]}, 1))
    caches = {rel: in_vmem(held[rel][0]) for rel in (0, 1)}
    spans = {rel: in_vmem(held[rel][1]) for rel in (0, 1)}
    near = [rel for rel in range(n_tok) if rel < 2]
    far = [rel for rel in range(n_tok) if rel >= 2]

    def key_scratch(rels):
        keys = len(rels) * (cache_rows + tokens)
        return [
            pltpu.VMEM((KQ, keys), bf16),
            pltpu.VMEM((keys, KVL), bf16),
        ]

    group = math.gcd(heads, 4)
    anywhere = pl.BlockSpec(memory_space=pltpu.HBM)
    q = in_vmem(
        pl.pallas_call(
            functools.partial(query_kernel, tokens, group),
            in_specs=[anywhere] * 3,
            out_specs=vmem,
            out_shape=pltpu.VMEM((CHUNKS, heads, rows, KQ), bf16),
            scratch_shapes=[
                pltpu.VMEM(q_nope.shape, bf16),
                pltpu.VMEM(q_rope.shape, bf16),
                pltpu.VMEM(w_uk.shape, bf16),
                pltpu.SemaphoreType.DMA((heads // group, 3)),
            ],
            compiler_params=params,
            name="query_latent",
            cost_estimate=cost(2 * tokens * w_uk.size),
        )(*[pltpu.with_memory_space_constraint(x, pltpu.HBM) for x in (q_nope, q_rope, w_uk)])
    )
    group = math.gcd(heads, 8)
    state = pl.pallas_call(
        functools.partial(local_kernel, near, tokens, group),
        in_specs=[smem] + [vmem] * (1 + 2 * len(near)),
        out_specs=[vmem] * 3,
        out_shape=[
            pltpu.VMEM((CHUNKS, heads, rows, KVL), f32),
            pltpu.VMEM((CHUNKS, heads, rows, LANES), f32),
            pltpu.VMEM((CHUNKS, heads, rows, LANES), f32),
        ],
        scratch_shapes=key_scratch(near),
        compiler_params=params,
        name="local_keys",
        cost_estimate=cost(4 * tokens * heads * len(near) * (cache_rows + tokens) * KD),
    )(prefix_length, q, *[caches[r] for r in near], *[spans[r] for r in near])
    others = {rel: both for rel, both in held.items() if rel > 1}
    others, state = lax.optimization_barrier((others, state))
    caches.update({rel: in_vmem(both[0]) for rel, both in others.items()})
    spans.update({rel: in_vmem(both[1]) for rel, both in others.items()})

    def go_on(which, rels, state, last):
        if last:
            shapes = [pltpu.VMEM((rows, heads * DV), bf16)]
        else:
            shapes = [
                pltpu.VMEM((1, heads, rows, KVL), f32),
                pltpu.VMEM((1, heads, rows, LANES), f32),
                pltpu.VMEM((1, heads, rows, LANES), f32),
            ]
        up = [in_vmem(w_uv)] if last else []
        return pl.pallas_call(
            functools.partial(step_kernel, rels, tokens, group, which, last),
            in_specs=[smem] + [vmem] * (4 + len(up) + 2 * len(rels)),
            out_specs=[vmem] * len(shapes),
            out_shape=shapes,
            scratch_shapes=key_scratch(rels),
            compiler_params=params,
            name="far_keys" if last else "counterpart_keys",
            cost_estimate=cost(4 * rows * heads * len(rels) * (cache_rows + tokens) * KD),
        )(
            prefix_length,
            q,
            *[in_vmem(x) for x in state],
            *up,
            *[caches[r] for r in rels],
            *[spans[r] for r in rels],
        )

    straight = [go_on(which, [r for r in far if r % 2 == 0], state, False) for which in range(AHEAD)]
    crossed = key_step(others, 1)
    if AHEAD:
        crossed, straight[0] = lax.optimization_barrier((crossed, straight[0]))
    caches.update({rel: in_vmem(both[0]) for rel, both in crossed.items()})
    spans.update({rel: in_vmem(both[1]) for rel, both in crossed.items()})

    def rest(which):
        if which < AHEAD:
            return go_on(which, [rel for rel in far if rel % 2], straight[which], True)[0]
        return go_on(which, far, state, True)[0]

    columns = w_o.shape[1]
    depth = w_o.shape[0]
    tile = 256 if columns % 256 == 0 else columns
    tiles = columns // tile
    groups, start = [], 0
    for at, (share, stages) in enumerate(PLAN):
        count = round(tiles * share)
        if at == len(PLAN) - 1:
            count = tiles - start
        if count > 0:
            groups.append((stages(bits_of(n_head)), start, count, tile))
            start += count

    def project(values):
        shapes = [
            pltpu.VMEM((n_head // ways * (rows // per), tile * count), bf16)
            for ways, count in (
                (len(combinations(stages[0])), count) for stages, _, count, _ in groups
            )
            for _ in range(ways)
        ]
        return pl.pallas_call(
            functools.partial(project_kernel, n_tok, per, groups),
            in_specs=[vmem] * (n_tok + 1),
            out_specs=[vmem] * len(shapes),
            out_shape=shapes,
            scratch_shapes=[pltpu.VMEM((n_head // per * rows, depth), bf16)],
            compiler_params=params,
            name="project",
            cost_estimate=cost(2 * n_head // per * rows * depth * columns),
        )(*values, in_vmem(w_o))

    def scatter(parts, stages):
        for at, bits in enumerate(stages):
            moves = combinations(bits)[:-1]
            got = [xor_permute(x, "head", move) for x, move in zip(parts, moves)]
            terms = [parts[-1]] + got
            if at + 1 < len(stages):
                ways = len(combinations(stages[at + 1]))
                size = terms[0].shape[0] // ways
                parts = [
                    sum(x[j * size : (j + 1) * size].astype(f32) for x in terms).astype(bf16)
                    for j in range(ways)
                ]
        return terms

    places, terms = [], []
    for which in range(CHUNKS):
        parts = list(project(gather(rest(which))))
        for stages, start, count, _ in groups:
            ways = len(combinations(stages[0]))
            found = scatter(parts[:ways], stages)
            places.append((which * (rows // per), start * tile, len(found)))
            terms += found
            parts = parts[ways:]
    return pl.pallas_call(
        functools.partial(join_kernel, places),
        in_specs=[vmem] * len(terms),
        out_specs=vmem,
        out_shape=jax.ShapeDtypeStruct((CHUNKS * (rows // per), columns), bf16),
        compiler_params=params,
        name="join",
    )(*[in_vmem(x) for x in terms])


def solution(mesh):
    return jax.shard_map(
        shards,
        mesh=mesh,
        in_specs=(
            P("tok", "head"),
            P("tok", "head"),
            P("tok", None),
            P("tok", None),
            P(None, "head"),
            P(None, "head"),
            P("head", "tok"),
            P(),
        ),
        out_specs=P("head", "tok"),
        check_vma=False,
    )
```
